32 devices in a mesh: fsdp: 4 (over y, core), dp: 4 (over z), engine: 2 (over x).
Axes of the slice: x: 2, y: 2, z: 4, core: 2. Of those that a mesh axis runs over, the one named last changes fastest.
Arguments:
- activations: bfloat16 [4096, 8192], P(('fsdp', 'dp', 'engine')), may hold values from -6 to 6
- upstream: bfloat16 [4096, 512], P(('fsdp', 'dp', 'engine')), may hold values from -6 to 6
- segment: int32 [32, 128], P(('fsdp', 'dp', 'engine')), may hold values from 0 to 3, never falling along the last dimension, each value on 1 to 64 neighbouring positions
- reward: float32 [128], P(('fsdp', 'dp', 'engine')), may hold values from -6 to 6
- prompt_group_index: int32 [128, 1], P(('fsdp', 'dp', 'engine')), may hold values from 0 to 7
- frozen_value_weight: bfloat16 [8192, 512], P(('fsdp', 'engine')), may hold values from -0.25 to 0.25
- adapter_down_weight: bfloat16 [8192, 64], P('fsdp'), may hold values from -0.0625 to 0.0625
- adapter_up_weight: bfloat16 [64, 512], replicated, may hold values from -0.75 to 0.75
Outputs:
- input_gradient: bfloat16 [4096, 8192], P(('fsdp', 'dp', 'engine'))
- step_down: float32 [8192, 64], P('fsdp')
- step_up: float32 [64, 512], replicated
The draws below stay inside these ranges and needn't reach their ends.
Inputs may be any that keep to these rules, and one draw needn't show every extreme that they name: `segment`: within each row the numbers never fall and every rollout 0 to 3 has at least one token. `prompt_group_index`: every group has at least one rollout.
All inputs are finite; a program needn't handle non-finite values.
Results may differ from the reference program's by a relative error of at most 0.011.
Values may be sent and summed in bfloat16 or wider, within the bound.
A program may use at most 64 MiB of HBM per device.

```python
import math
import jax
import jax.numpy as jnp
import numpy as np
from jax import lax

MODEL_WIDTH = 8192
VALUE_OUTPUTS = 512
ADAPTER_RANK = 64
TOK_DEV = 128
SEQ_DEV = 4
TOKENS = 4096
SEQS = 128
GROUPS = 8
N_FSDP = 4
N_DP = 4
N_ENGINE = 2
DEVICES = 32


def steps_of(stream_key, dims, split, smallest, high):
    level = 1.0
    for axis_at, blocks in split:
        steps = jax.random.uniform(jax.random.fold_in(jax.random.fold_in(stream_key, 6), axis_at), (blocks,), jnp.float32, smallest / len(split), high / len(split))
        level = level * jnp.repeat(jnp.exp(steps), dims[axis_at] // blocks).reshape((-1,) + (1,) * (len(dims) - 1 - axis_at))
    return level


def choose_distinct(rng, rows, number_of, top, lift):
    order = jax.random.permutation(jax.random.fold_in(rng, 1), number_of)
    boost = order
    for power in range(3):
        boost = boost * boost // number_of
    boost = boost * lift // number_of
    chance = jax.random.randint(jax.random.fold_in(rng, 2), (rows, number_of), 0, 4096) + boost
    fixed_rows = jax.random.permutation(jax.random.fold_in(rng, 3), rows)[jnp.arange(number_of) % rows]
    chance = jnp.where(jnp.arange(rows)[:, None] == fixed_rows[None, :], 1 << 14, chance)
    merit = chance * number_of + jnp.arange(number_of)
    return lax.top_k(merit.astype(jnp.int32), top)[1].astype(jnp.int32)


def length_profile(amount, total, reach, slope):
    portions = [(1 << 20) // math.isqrt(rank ** slope) + 1 for rank in range(2, amount + 1)]
    surplus, given = total - reach - (amount - 1), [1] * (amount - 1)
    while surplus > 0:
        candidates = [i for i in range(amount - 1) if given[i] < reach]
        mass, remaining = sum([portions[i] for i in candidates]), surplus
        for i in candidates:
            extra = min(reach - given[i], max(1, remaining * portions[i] // mass), surplus)
            given[i] = given[i] + extra
            surplus = surplus - extra
    return np.array([reach] + given)


def ragged(key, amount, total, limit, slope):
    if amount == 2:
        one = jax.random.randint(key, (), max(1, total - limit), min(limit, total - 1) + 1)
        return jnp.stack([one, total - one])
    sizes = jnp.asarray(length_profile(amount, total, limit, slope), jnp.int32)
    pairs = (amount - 1) // 2
    source_of, taker = sizes[1:1 + 2 * pairs:2], sizes[2:2 + 2 * pairs:2]
    room = jnp.minimum(source_of - 1, limit - taker)
    moved = jax.random.randint(jax.random.fold_in(key, 1), (pairs,), 0, 1 << 20) % (room + 1)
    sizes = sizes.at[1:1 + 2 * pairs:2].set(source_of - moved).at[2:2 + 2 * pairs:2].set(taker + moved)
    return sizes[jax.random.permutation(jax.random.fold_in(key, 2), amount)]


def gaussian(own_key, shape, spread, bound, shards=(), held_as=jnp.bfloat16):
    level = steps_of(own_key, shape, shards, -0.22, 0.18) if shards else 1.0
    array = jax.random.normal(own_key, shape, jnp.float32) * spread * level
    return jnp.minimum(jnp.maximum(array, -bound), bound).astype(held_as)


def setup_inputs(seed: int = 0) -> dict:
    streams_of = jax.random.split(jax.random.key(seed), 9)
    return {
        "activations": gaussian(streams_of[0], (TOKENS, MODEL_WIDTH), 1.0, 6.0, ((0, 32),)),
        "upstream": gaussian(streams_of[1], (TOKENS, VALUE_OUTPUTS), 1.0, 6.0, ((0, 32),)),
        "segment": jax.vmap(lambda own: jnp.searchsorted(jnp.cumsum(ragged(own, SEQ_DEV, TOK_DEV, TOK_DEV // 2, 2)), jnp.arange(TOK_DEV), side="right"))(jax.random.split(streams_of[2], DEVICES)).reshape((DEVICES, TOK_DEV)).astype(jnp.int32),
        "reward": gaussian(streams_of[3], (SEQS,), 1.0, 6.0, ((0, 32),), jnp.float32),
        "prompt_group_index": choose_distinct(streams_of[4], SEQS, GROUPS, 1, 0),
        "frozen_value_weight": gaussian(streams_of[5], (MODEL_WIDTH, VALUE_OUTPUTS), VALUE_OUTPUTS ** -0.5, 0.25, ((0, 8),)),
        "adapter_down_weight": gaussian(streams_of[6], (MODEL_WIDTH, ADAPTER_RANK), MODEL_WIDTH ** -0.5, 0.0625, ((0, 4),)),
        "adapter_up_weight": gaussian(streams_of[7], (ADAPTER_RANK, VALUE_OUTPUTS), ADAPTER_RANK ** -0.5, 0.75),
    }


adapter_scale = 2.0
HIGH = lax.Precision.HIGHEST

def reference(activations, upstream, segment, reward, prompt_group_index, frozen_value_weight, adapter_down_weight, adapter_up_weight):
    device_count = N_FSDP * N_DP * N_ENGINE
    labels = jnp.arange(GROUPS, dtype=jnp.int32)
    member = (prompt_group_index[:, 0:1] == labels[None, :]).astype(jnp.float32)
    group_sum = jnp.dot(reward, member, precision=HIGH)
    group_count = lax.optimization_barrier(jnp.sum(member, axis=0))
    advantage = reward - jnp.dot(member, group_sum / group_count, precision=HIGH)
    block_adv = advantage.reshape(device_count, SEQ_DEV)
    act_blocks = activations.reshape(device_count, TOK_DEV, MODEL_WIDTH)
    upper_blocks = upstream.reshape(device_count, TOK_DEV, VALUE_OUTPUTS)
    seq_ids = jnp.arange(SEQ_DEV, dtype=jnp.int32)
    contract_trailing = (((1,), (1,)), ((), ()))
    contract_leading = (((0,), (0,)), ((), ()))

    def one_block(carry, items):
        down_gradient, up_gradient = carry
        activation_rows, upper, seg_row, adv_row = items
        token_member = (seg_row[:, None] == seq_ids[None, :]).astype(jnp.float32)
        token_adv = jnp.dot(token_member, adv_row, precision=HIGH)
        advantage_weighted = (upper.astype(jnp.float32) * token_adv[:, None]).astype(jnp.bfloat16)
        lowrank_activation = jnp.dot(activation_rows, adapter_down_weight, preferred_element_type=jnp.float32).astype(jnp.bfloat16)
        backward_lowrank = lax.dot_general(advantage_weighted, adapter_up_weight, contract_trailing, preferred_element_type=jnp.float32).astype(jnp.bfloat16)
        frozen_gradient = lax.dot_general(advantage_weighted, frozen_value_weight, contract_trailing, preferred_element_type=jnp.float32).astype(jnp.bfloat16)
        adapter_portion = lax.dot_general(backward_lowrank, adapter_down_weight, contract_trailing, preferred_element_type=jnp.float32)
        gradient_block = (frozen_gradient.astype(jnp.float32) + adapter_scale * adapter_portion).astype(jnp.bfloat16)
        down_contribution = adapter_scale * lax.dot_general(activation_rows, backward_lowrank, contract_leading, preferred_element_type=jnp.float32)
        up_contribution = adapter_scale * lax.dot_general(lowrank_activation, advantage_weighted, contract_leading, preferred_element_type=jnp.float32)
        return ((down_gradient + down_contribution, up_gradient + up_contribution), gradient_block)
    start = (jnp.zeros((MODEL_WIDTH, ADAPTER_RANK), jnp.float32), jnp.zeros((ADAPTER_RANK, VALUE_OUTPUTS), jnp.float32))
    (down_gradient, up_gradient), grad_blocks = lax.scan(one_block, start, (act_blocks, upper_blocks, segment, block_adv))
    input_gradient = grad_blocks.reshape(TOKENS, MODEL_WIDTH)
    grad_norm = jnp.sqrt(jnp.sum(down_gradient * down_gradient) + jnp.sum(up_gradient * up_gradient))
    clip_norm = jnp.sqrt(jnp.float32(MODEL_WIDTH * ADAPTER_RANK + ADAPTER_RANK * VALUE_OUTPUTS))
    factor = jnp.minimum(jnp.float32(1.0), clip_norm / (grad_norm + 1e-06))
    return (input_gradient, factor * down_gradient, factor * up_gradient)
```

```python
import functools

import jax
import jax.numpy as jnp
from jax import lax
from jax.experimental import pallas as pl
from jax.experimental.pallas import tpu as pltpu
from jax.sharding import PartitionSpec as P

GSIZE = 16
LANES = 128
SCALE = 2.0
MESH = pl.DeviceIdType.MESH
TRAILING = (((1,), (1,)), ((), ()))
F32 = jnp.float32
BF16 = jnp.bfloat16


def kernel(
    dims,
    act_hbm,
    ups_ref,
    info_ref,
    w_hbm,
    down_ref,
    upw_ref,
    out_hbm,
    sd_ref,
    su_ref,
    act,
    w,
    zinfo,
    pinfo,
    adv,
    uall,
    dall,
    wown,
    gsend,
    grecv,
    usend,
    urecv,
    zs,
    zu,
    fin,
    fu,
    stage,
    load_sem,
    zinfo_s,
    zinfo_r,
    pinfo_s,
    pinfo_r,
    u_s,
    u_r,
    d_s,
    d_r,
    g_s,
    g_r,
    up_s,
    up_r,
    zs_s,
    zs_r,
    zu_s,
    zu_r,
    fin_s,
    fin_r,
    fu_s,
    fu_r,
    out_s,
    out_r,
):
    nf, nd, ne, seqs, groups = dims
    np_ = nf * ne
    f, d, e = lax.axis_index("fsdp"), lax.axis_index("dp"), lax.axis_index("engine")
    p = f * ne + e
    cols = w.shape[0]
    rank, values = upw_ref.shape
    chunks = rank // 8

    def each(count, fn):
        if count <= 8:
            for s in range(1, count):
                fn(s)
        else:

            @pl.loop(1, count)
            def _(s):
                fn(s)

    def plane(s):
        q = lax.rem(p + s, np_)
        return q, {"fsdp": q // ne, "engine": lax.rem(q, ne)}

    def line(s):
        q = lax.rem(d + s, nd)
        return q, {"dp": q}

    def fs(s):
        q = lax.rem(f + s, nf)
        return q, {"fsdp": q}

    def eng(s):
        q = lax.rem(e + s, ne)
        return q, {"engine": q}

    def copy(src, dst, ss, rs, dev):
        return pltpu.make_async_remote_copy(
            src_ref=src, dst_ref=dst, send_sem=ss, recv_sem=rs, device_id=dev, device_id_type=MESH
        )

    def span(q, width):
        return pl.ds(pl.multiple_of(q * width, LANES), width)

    load_act = pltpu.make_async_copy(act_hbm, act, load_sem.at[0])
    load_w = pltpu.make_async_copy(w_hbm, w, load_sem.at[1])
    load_act.start()
    load_w.start()

    barrier = pltpu.get_barrier_semaphore()
    each(nd, lambda s: pl.semaphore_signal(barrier, inc=1, device_id=line(s)[1], device_id_type=MESH))
    each(np_, lambda s: pl.semaphore_signal(barrier, inc=1, device_id=plane(s)[1], device_id_type=MESH))
    pl.semaphore_wait(barrier, nd - 1 + np_ - 1)

    def send(peers, count, src, dst, ss, rs, me):
        def go(s):
            q, dev = peers(s)
            copy(src(q), dst(me), ss.at[q], rs.at[me], dev).start()

        each(count, go)

    def arrive(peers, count, src, dst, ss, rs):
        def go(s):
            q, dev = peers(s)
            copy(src(q), dst(q), ss.at[q], rs.at[q], dev).wait_recv()

        each(count, go)

    def sent(peers, count, src, dst, ss, rs, me):
        def go(s):
            q, dev = peers(s)
            copy(src(q), dst(me), ss.at[q], rs.at[me], dev).wait_send()

        each(count, go)

    zi = (line, nd, lambda q: info_ref, lambda q: zinfo.at[q], zinfo_s, zinfo_r)
    pi = (plane, np_, lambda q: zinfo, lambda q: pinfo.at[q], pinfo_s, pinfo_r)
    ua = (plane, np_, lambda q: ups_ref, lambda q: uall.at[q], u_s, u_r)
    da = (fs, nf, lambda q: down_ref, lambda q: dall.at[q], d_s, d_r)
    gr = (plane, np_, lambda q: gsend.at[q], lambda q: grecv.at[q], g_s, g_r)
    ur = (plane, np_, lambda q: usend.at[q], lambda q: urecv.at[q], up_s, up_r)
    zg = (line, nd, lambda q: zs.at[d], lambda q: zs.at[q], zs_s, zs_r)
    zp = (line, nd, lambda q: zu.at[d], lambda q: zu.at[q], zu_s, zu_r)
    fg = (eng, ne, lambda q: fin.at[e], lambda q: fin.at[q], fin_s, fin_r)
    fp = (plane, np_, lambda q: fu.at[p], lambda q: fu.at[q], fu_s, fu_r)
    og = (plane, np_, lambda q: stage.at[q], lambda q: out_hbm.at[:, span(q, cols)], out_s, out_r)

    send(*zi, d)
    zinfo[d] = info_ref[...]
    arrive(*zi)
    send(*pi, p)
    send(*ua, p)
    send(*da, f)
    pinfo[p] = zinfo[...]
    uall[p] = ups_ref[...]
    dall[f] = down_ref[...]
    arrive(*pi)

    rewards = pinfo[:, :, 0, :]
    labels = pinfo[:, :, 1, :]

    def group_mean(g, mean):
        hit = labels == jnp.asarray(g, F32)
        total = jnp.sum(jnp.where(hit, rewards, 0.0), axis=(0, 1, 2), keepdims=True)
        number = jnp.sum(jnp.where(hit, 1.0, 0.0), axis=(0, 1, 2), keepdims=True)
        return jnp.where(hit, total / number, mean)

    mean = jnp.zeros(rewards.shape, F32)
    if groups <= 8:
        for g in range(groups):
            mean = group_mean(g, mean)
    else:
        mean = lax.fori_loop(0, groups, group_mean, mean)
    adv[...] = rewards - mean

    tok = ups_ref.shape[0]
    eye = lax.broadcasted_iota(jnp.int32, (tok, tok), 0) == lax.broadcasted_iota(
        jnp.int32, (tok, tok), 1
    )

    def weigh(q):
        seg = pinfo[q, d, 2:3, :]
        of_seq = adv[q, pl.ds(d, 1), :]
        row = jnp.zeros((1, tok), F32)
        for s in range(seqs):
            row = jnp.where(seg == s, of_seq[:, s : s + 1], row)
        col = jnp.sum(jnp.where(eye, row, 0.0), axis=1, keepdims=True)
        return (uall[q].astype(F32) * col).astype(BF16)

    def dot_nt(a, b):
        return lax.dot_general(a, b, TRAILING, preferred_element_type=F32)

    own = weigh(p)
    wown[...] = own
    back_t = dot_nt(upw_ref[...], own).astype(BF16)
    load_act.wait()

    def grad_block(q):
        part = SCALE * jnp.dot(back_t, act[:, span(q, cols)], preferred_element_type=F32)
        return part.astype(BF16)

    @pl.loop(1, np_)
    def _(s):
        q, dev = plane(s)
        gsend[q] = grad_block(q)
        copy(gsend.at[q], grecv.at[p], g_s.at[q], g_r.at[p], dev).start()

    grecv[p] = grad_block(p)
    load_w.wait()

    def grad_in(q):
        mine = weigh(q)
        back = dot_nt(mine, upw_ref[...]).astype(BF16)
        base = dot_nt(mine, w[...]).astype(BF16)
        adapter = jnp.dot(back, down_ref[:, span(e, cols)], preferred_element_type=F32)
        return (base.astype(F32) + SCALE * adapter).astype(BF16)

    @pl.loop(1, np_)
    def _(s):
        q, dev = plane(s)
        copy(ups_ref, uall.at[q], u_s.at[q], u_r.at[q], dev).wait_recv()
        stage[q] = grad_in(q)
        copy(stage.at[q], out_hbm.at[:, span(p, cols)], out_s.at[q], out_r.at[p], dev).start()

    stage[p] = grad_in(p)
    keep = pltpu.make_async_copy(stage.at[p], out_hbm.at[:, span(p, cols)], load_sem.at[2])
    keep.start()

    arrive(*da)
    width = down_ref.shape[1]
    low_t = lax.fori_loop(
        0,
        nf,
        lambda i, acc: acc + dot_nt(dall[i], act[:, span(i, width)]),
        jnp.zeros((rank, tok), F32),
    ).astype(BF16)
    part = SCALE * jnp.dot(low_t, wown[...], preferred_element_type=F32)
    if np_ > chunks:
        usend[...] = jnp.zeros(usend.shape, F32)
    usend[0:chunks] = part.reshape(chunks, 8, values)
    send(*ur, p)
    urecv[p] = usend[p]

    arrive(*gr)
    zs[d] = lax.fori_loop(
        0, np_, lambda i, acc: acc + grecv[i].astype(F32), jnp.zeros((rank, cols), F32)
    ).astype(BF16)
    send(*zg, d)
    arrive(*ur)
    zu[d] = lax.fori_loop(0, np_, lambda i, acc: acc + urecv[i], jnp.zeros((8, values), F32))
    send(*zp, d)
    arrive(*zg)
    total = jnp.zeros((rank, cols), F32)
    for i in range(nd):
        total = total + zs[i].astype(F32)
    fin[e] = total.astype(BF16)
    send(*fg, e)
    arrive(*zp)
    up_total = jnp.zeros((8, values), F32)
    for i in range(nd):
        up_total = up_total + zu[i]
    square = jnp.sum(total * total, axis=(0, 1), keepdims=True) + jnp.sum(
        up_total * up_total, axis=(0, 1), keepdims=True
    )
    fu[p, :, 0:values] = up_total
    fu[p, :, values:] = jnp.broadcast_to(square, (8, LANES))
    send(*fp, p)

    arrive(*fp)
    squares = jnp.sum(fu[:, 0:1, values : values + 1], axis=0)
    count = F32(rank * act.shape[1] + rank * values)
    factor = jnp.minimum(F32(1.0), jnp.sqrt(count) / (jnp.sqrt(squares) + F32(1e-6)))
    su_ref[...] = fu[0:chunks, :, 0:values].reshape(rank, values) * factor
    arrive(*fg)
    for i in range(ne):
        sd_ref[:, i * cols : (i + 1) * cols] = fin[i].astype(F32) * factor

    keep.wait()
    arrive(*og)
    sent(*zi, d)
    sent(*pi, p)
    sent(*ua, p)
    sent(*da, f)
    sent(*gr, p)
    sent(*ur, p)
    sent(*zg, d)
    sent(*zp, d)
    sent(*fg, e)
    sent(*fp, p)
    sent(*og, p)


def local(
    activations,
    upstream,
    segment,
    reward,
    prompt_group_index,
    frozen_value_weight,
    adapter_down_weight,
    adapter_up_weight,
):
    nf, nd, ne = lax.axis_size("fsdp"), lax.axis_size("dp"), lax.axis_size("engine")
    np_ = nf * ne
    seqs = reward.shape[0]
    groups = seqs * nf * nd * ne // GSIZE
    tok, model = activations.shape
    values = upstream.shape[1]
    cols = frozen_value_weight.shape[0]
    width, rank = adapter_down_weight.shape

    def line(x, fill):
        return jnp.pad(x.astype(F32).reshape(1, -1), ((0, 0), (0, LANES - x.size)), constant_values=fill)

    info = jnp.concatenate(
        [line(reward, 0.0), line(prompt_group_index, -1.0), line(segment, 0.0), jnp.zeros((5, LANES), F32)]
    )
    vmem = pl.BlockSpec(memory_space=pltpu.VMEM)
    anym = pl.BlockSpec(memory_space=pl.ANY)
    dma = pltpu.SemaphoreType.DMA
    plane2 = [dma((np_,)), dma((np_,))]
    line2 = [dma((nd,)), dma((nd,))]
    out, sd, su = pl.pallas_call(
        functools.partial(kernel, (nf, nd, ne, seqs, groups)),
        out_shape=(
            jax.ShapeDtypeStruct((tok, model), BF16),
            jax.ShapeDtypeStruct((rank, width), F32),
            jax.ShapeDtypeStruct((rank, values), F32),
        ),
        in_specs=[anym, vmem, vmem, anym, vmem, vmem],
        out_specs=(anym, vmem, vmem),
        scratch_shapes=[
            pltpu.VMEM((tok, model), BF16),
            pltpu.VMEM((cols, values), BF16),
            pltpu.VMEM((nd, 8, LANES), F32),
            pltpu.VMEM((np_, nd, 8, LANES), F32),
            pltpu.VMEM((np_, nd, LANES), F32),
            pltpu.VMEM((np_, tok, values), BF16),
            pltpu.VMEM((nf, rank, width), BF16),
            pltpu.VMEM((tok, values), BF16),
            pltpu.VMEM((np_, rank, cols), BF16),
            pltpu.VMEM((np_, rank, cols), BF16),
            pltpu.VMEM((np_, 8, values), F32),
            pltpu.VMEM((np_, 8, values), F32),
            pltpu.VMEM((nd, rank, cols), BF16),
            pltpu.VMEM((nd, 8, values), F32),
            pltpu.VMEM((ne, rank, cols), BF16),
            pltpu.VMEM((np_, 8, values + LANES), F32),
            pltpu.VMEM((np_, tok, cols), BF16),
            dma((3,)),
        ]
        + line2
        + plane2
        + plane2
        + [dma((nf,)), dma((nf,))]
        + plane2
        + plane2
        + line2
        + line2
        + [dma((ne,)), dma((ne,))]
        + plane2
        + plane2,
        compiler_params=pltpu.CompilerParams(
            collective_id=0, has_side_effects=True, vmem_limit_bytes=48 * 1024 * 1024
        ),
        cost_estimate=pl.CostEstimate(
            flops=4 * tok * model * values, bytes_accessed=6 * tok * model, transcendentals=0
        ),
    )(activations, upstream, info, frozen_value_weight, adapter_down_weight.T, adapter_up_weight)
    return out, sd.T, su


def solution(mesh):
    everything = ("fsdp", "dp", "engine")
    return jax.shard_map(
        local,
        mesh=mesh,
        in_specs=(
            P(everything, None),
            P(everything, None),
            P(everything, None),
            P(everything),
            P(everything, None),
            P(("fsdp", "engine"), None),
            P("fsdp", None),
            P(),
        ),
        out_specs=(P(everything, None), P("fsdp", None), P()),
        check_vma=False,
    )
```

```python
import functools

import jax
import jax.numpy as jnp
from jax import lax
from jax.experimental import pallas as pl
from jax.experimental.pallas import tpu as pltpu
from jax.sharding import PartitionSpec as P

GSIZE = 16
LANES = 128
SCALE = 2.0
MESH = pl.DeviceIdType.MESH
TRAILING = (((1,), (1,)), ((), ()))
F32 = jnp.float32
BF16 = jnp.bfloat16


def kernel(
    dims,
    act_hbm,
    ups_hbm,
    reward_ref,
    group_ref,
    seg_ref,
    w_hbm,
    down_hbm,
    upw_hbm,
    out_hbm,
    sd_ref,
    su_ref,
    act,
    w,
    upw_ref,
    zinfo,
    pinfo,
    adv,
    uall,
    dall,
    wown,
    gsend,
    gmate,
    grecv,
    usend,
    umate,
    urecv,
    zs,
    zu,
    fin,
    fu,
    stage,
    load_sem,
    zinfo_s,
    zinfo_r,
    pinfo_s,
    pinfo_r,
    u_s,
    u_r,
    d_s,
    d_r,
    gm_s,
    gm_r,
    g_s,
    g_r,
    um_s,
    um_r,
    up_s,
    up_r,
    zs_s,
    zs_r,
    zu_s,
    zu_r,
    fin_s,
    fin_r,
    fu_s,
    fu_r,
    out_s,
    out_r,
):
    nf, nd, ne, seqs, groups = dims
    np_ = nf * ne
    f, d, e = lax.axis_index("fsdp"), lax.axis_index("dp"), lax.axis_index("engine")
    p = f * ne + e
    half = np_ // 2
    fb = lax.rem(f, 2)
    h = (f // 2) * ne + e
    other = 1 - 2 * fb
    sib = {"fsdp": f + other}
    cols = w.shape[0]
    rank, values = upw_ref.shape
    chunks = rank // 8

    def each(count, fn):
        if count <= 8:
            for s in range(1, count):
                fn(s)
        else:

            @pl.loop(1, count)
            def _(s):
                fn(s)

    def plane(s):
        q = lax.rem(p + s, np_)
        return q, {"fsdp": q // ne, "engine": lax.rem(q, ne)}

    def line(s):
        q = lax.rem(d + s, nd)
        return q, {"dp": q}

    def same(s):
        k = lax.rem(h + s, half)
        g = 2 * (k // ne) + fb
        return g * ne + lax.rem(k, ne), {"fsdp": g, "engine": lax.rem(k, ne)}

    def mate(q):
        return q + other * ne

    def fs(s):
        q = 2 * lax.rem(f // 2 + s, nf // 2) + fb
        return q, {"fsdp": q}

    def eng(s):
        q = lax.rem(e + s, ne)
        return q, {"engine": q}

    def copy(src, dst, ss, rs, dev):
        return pltpu.make_async_remote_copy(
            src_ref=src, dst_ref=dst, send_sem=ss, recv_sem=rs, device_id=dev, device_id_type=MESH
        )

    def span(q, width):
        return pl.ds(pl.multiple_of(q * width, LANES), width)

    def load(src, dst, i):
        got = pltpu.make_async_copy(src, dst, load_sem.at[i])
        got.start()
        return got

    load_ups = load(ups_hbm, uall.at[p], 3)
    load_upw = load(upw_hbm, upw_ref, 4)
    load_act = load(act_hbm, act, 0)
    load_down = load(down_hbm, dall.at[f], 5)
    load_w = load(w_hbm, w, 1)

    zinfo[d] = jnp.zeros(zinfo.shape[1:], F32)
    zinfo[d, 0:1, 0:seqs] = reward_ref[...]
    zinfo[d, 1:2, :] = jnp.full((1, LANES), -1.0, F32)
    zinfo[d, 1:2, 0:seqs] = group_ref[...].astype(F32)
    zinfo[d, 2:3, :] = seg_ref[...].astype(F32)

    barrier = pltpu.get_barrier_semaphore()
    each(nd, lambda s: pl.semaphore_signal(barrier, inc=1, device_id=line(s)[1], device_id_type=MESH))
    each(np_, lambda s: pl.semaphore_signal(barrier, inc=1, device_id=plane(s)[1], device_id_type=MESH))
    pl.semaphore_wait(barrier, nd - 1 + np_ - 1)

    def send(peers, count, src, dst, ss, rs, me):
        def go(s):
            q, dev = peers(s)
            copy(src(q), dst(me), ss.at[q], rs.at[me], dev).start()

        each(count, go)

    def arrive(peers, count, src, dst, ss, rs):
        def go(s):
            q, dev = peers(s)
            copy(src(q), dst(q), ss.at[q], rs.at[q], dev).wait_recv()

        each(count, go)

    def sent(peers, count, src, dst, ss, rs, me):
        def go(s):
            q, dev = peers(s)
            copy(src(q), dst(me), ss.at[q], rs.at[me], dev).wait_send()

        each(count, go)

    zi = (line, nd, lambda q: zinfo.at[d], lambda q: zinfo.at[q], zinfo_s, zinfo_r)
    pi = (plane, np_, lambda q: zinfo, lambda q: pinfo.at[q], pinfo_s, pinfo_r)
    ua = (same, half, lambda q: uall.at[p], lambda q: uall.at[q], u_s, u_r)
    da = (fs, nf // 2, lambda q: dall.at[f], lambda q: dall.at[q], d_s, d_r)
    gr = (same, half, lambda q: gsend.at[q], lambda q: grecv.at[q], g_s, g_r)
    ur = (same, half, lambda q: usend.at[q], lambda q: urecv.at[q], up_s, up_r)
    zg = (line, nd, lambda q: zs.at[d], lambda q: zs.at[q], zs_s, zs_r)
    zp = (line, nd, lambda q: zu.at[d], lambda q: zu.at[q], zu_s, zu_r)
    fg = (eng, ne, lambda q: fin.at[e], lambda q: fin.at[q], fin_s, fin_r)
    fp = (plane, np_, lambda q: fu.at[p], lambda q: fu.at[q], fu_s, fu_r)
    og = (plane, np_, lambda q: stage.at[q], lambda q: out_hbm.at[:, span(q, cols)], out_s, out_r)

    def hand_up(q):
        return copy(uall.at[q], uall.at[q], u_s.at[mate(q)], u_r.at[q], sib)

    def hand_down(g):
        return copy(dall.at[g], dall.at[g], d_s.at[g + other], d_r.at[g], sib)

    def hand_grad(q):
        return copy(gsend.at[q], gmate.at[q], gm_s.at[q], gm_r.at[q], sib)

    def hand_part(q):
        return copy(usend.at[q], umate.at[q], um_s.at[q], um_r.at[q], sib)

    send(*zi, d)
    arrive(*zi)
    send(*pi, p)
    load_ups.wait()
    send(*ua, p)
    hand_up(p).start()
    load_down.wait()
    send(*da, f)
    hand_down(f).start()
    pinfo[p] = zinfo[...]
    arrive(*pi)

    rewards = pinfo[:, :, 0, :]
    labels = pinfo[:, :, 1, :]

    def group_mean(g, mean):
        hit = labels == jnp.asarray(g, F32)
        total = jnp.sum(jnp.where(hit, rewards, 0.0), axis=(0, 1, 2), keepdims=True)
        number = jnp.sum(jnp.where(hit, 1.0, 0.0), axis=(0, 1, 2), keepdims=True)
        return jnp.where(hit, total / number, mean)

    mean = jnp.zeros(rewards.shape, F32)
    if groups <= 8:
        for g in range(groups):
            mean = group_mean(g, mean)
    else:
        mean = lax.fori_loop(0, groups, group_mean, mean)
    adv[...] = rewards - mean

    tok = act.shape[0]
    eye = lax.broadcasted_iota(jnp.int32, (tok, tok), 0) == lax.broadcasted_iota(
        jnp.int32, (tok, tok), 1
    )

    def weigh(q):
        seg = pinfo[q, d, 2:3, :]
        of_seq = adv[q, pl.ds(d, 1), :]
        row = jnp.zeros((1, tok), F32)
        for s in range(seqs):
            row = jnp.where(seg == s, of_seq[:, s : s + 1], row)
        col = jnp.sum(jnp.where(eye, row, 0.0), axis=1, keepdims=True)
        return (uall[q].astype(F32) * col).astype(BF16)

    def dot_nt(a, b):
        return lax.dot_general(a, b, TRAILING, preferred_element_type=F32)

    own = weigh(p)
    wown[...] = own
    load_upw.wait()
    back_t = dot_nt(upw_ref[...], own).astype(BF16)
    load_act.wait()

    def grad_block(q):
        return SCALE * jnp.dot(back_t, act[:, span(q, cols)], preferred_element_type=F32)

    @pl.loop(1, half + 1)
    def _(s):
        q = mate(same(s)[0])
        gsend[q] = grad_block(q).astype(BF16)
        hand_grad(q).start()

    def chip_block(q):
        part = grad_block(q)
        hand_grad(q).wait_recv()
        return (part + gmate[q].astype(F32)).astype(BF16)

    @pl.loop(1, half)
    def _(s):
        q, dev = same(s)
        gsend[q] = chip_block(q)
        copy(gsend.at[q], grecv.at[p], g_s.at[q], g_r.at[p], dev).start()

    grecv[p] = chip_block(p)
    load_w.wait()

    def grad_in(q):
        mine = weigh(q)
        back = dot_nt(mine, upw_ref[...]).astype(BF16)
        base = dot_nt(mine, w[...]).astype(BF16)
        adapter = jnp.dot(back, dall[f, :, span(e, cols)], preferred_element_type=F32)
        return (base.astype(F32) + SCALE * adapter).astype(BF16)

    def send_in(q, dev):
        stage[q] = grad_in(q)
        copy(stage.at[q], out_hbm.at[:, span(p, cols)], out_s.at[q], out_r.at[p], dev).start()

    @pl.loop(1, half)
    def _(s):
        q, dev = same(s)
        copy(uall.at[p], uall.at[q], u_s.at[q], u_r.at[q], dev).wait_recv()
        hand_up(q).start()
        send_in(q, dev)

    def pass_down(s):
        g, dev = fs(s)
        copy(dall.at[f], dall.at[g], d_s.at[g], d_r.at[g], dev).wait_recv()
        hand_down(g).start()

    each(nf // 2, pass_down)

    @pl.loop(1, half + 1)
    def _(s):
        q, dev = same(s)
        hand_up(mate(q)).wait_recv()
        send_in(mate(q), {"fsdp": dev["fsdp"] + other, "engine": dev["engine"]})

    stage[p] = grad_in(p)
    keep = pltpu.make_async_copy(stage.at[p], out_hbm.at[:, span(p, cols)], load_sem.at[2])
    keep.start()

    hand_down(f + other).wait_recv()
    each(nf // 2, lambda s: hand_down(fs(s)[0] + other).wait_recv())
    width = dall.shape[2]
    low_t = lax.fori_loop(
        0,
        nf,
        lambda i, acc: acc + dot_nt(dall[i], act[:, span(i, width)]),
        jnp.zeros((rank, tok), F32),
    ).astype(BF16)
    part = SCALE * jnp.dot(low_t, wown[...], preferred_element_type=F32)
    if np_ > chunks:
        usend[...] = jnp.zeros(usend.shape, F32)
    usend[0:chunks] = part.reshape(chunks, 8, values)
    @pl.loop(1, half + 1)
    def _(s):
        hand_part(mate(same(s)[0])).start()

    @pl.loop(1, half)
    def _(s):
        q, dev = same(s)
        hand_part(q).wait_recv()
        usend[q] = usend[q] + umate[q]
        copy(usend.at[q], urecv.at[p], up_s.at[q], up_r.at[p], dev).start()

    hand_part(p).wait_recv()
    urecv[p] = usend[p] + umate[p]

    def peer(k):
        return (2 * (k // ne) + fb) * ne + lax.rem(k, ne)

    arrive(*gr)
    zs[d] = lax.fori_loop(
        0, half, lambda i, acc: acc + grecv[peer(i)].astype(F32), jnp.zeros((rank, cols), F32)
    ).astype(BF16)
    send(*zg, d)
    arrive(*ur)
    zu[d] = lax.fori_loop(0, half, lambda i, acc: acc + urecv[peer(i)], jnp.zeros((8, values), F32))
    send(*zp, d)
    arrive(*zg)
    total = jnp.zeros((rank, cols), F32)
    for i in range(nd):
        total = total + zs[i].astype(F32)
    fin[e] = total.astype(BF16)
    send(*fg, e)
    arrive(*zp)
    up_total = jnp.zeros((8, values), F32)
    for i in range(nd):
        up_total = up_total + zu[i]
    square = jnp.sum(total * total, axis=(0, 1), keepdims=True) + jnp.sum(
        up_total * up_total, axis=(0, 1), keepdims=True
    )
    fu[p, :, 0:values] = up_total
    fu[p, :, values:] = jnp.broadcast_to(square, (8, LANES))
    send(*fp, p)

    arrive(*fp)
    squares = jnp.sum(fu[:, 0:1, values : values + 1], axis=0)
    count = F32(rank * act.shape[1] + rank * values)
    factor = jnp.minimum(F32(1.0), jnp.sqrt(count) / (jnp.sqrt(squares) + F32(1e-6)))
    su_ref[...] = fu[0:chunks, :, 0:values].reshape(rank, values) * factor
    arrive(*fg)
    for i in range(ne):
        sd_ref[:, i * cols : (i + 1) * cols] = fin[i].astype(F32) * factor

    keep.wait()
    arrive(*og)
    sent(*zi, d)
    sent(*pi, p)
    sent(*ua, p)
    sent(*da, f)
    sent(*gr, p)
    sent(*ur, p)

    @pl.loop(0, half)
    def _(s):
        q = same(s)[0]
        hand_up(q).wait_send()
        hand_grad(mate(q)).wait_send()
        hand_part(mate(q)).wait_send()

    @pl.loop(0, nf // 2)
    def _(s):
        hand_down(fs(s)[0]).wait_send()

    sent(*zg, d)
    sent(*zp, d)
    sent(*fg, e)
    sent(*fp, p)
    sent(*og, p)


def local(
    activations,
    upstream,
    segment,
    reward,
    prompt_group_index,
    frozen_value_weight,
    adapter_down_weight,
    adapter_up_weight,
):
    nf, nd, ne = lax.axis_size("fsdp"), lax.axis_size("dp"), lax.axis_size("engine")
    np_ = nf * ne
    seqs = reward.shape[0]
    groups = seqs * nf * nd * ne // GSIZE
    tok, model = activations.shape
    values = upstream.shape[1]
    cols = frozen_value_weight.shape[0]
    width, rank = adapter_down_weight.shape

    vmem = pl.BlockSpec(memory_space=pltpu.VMEM)
    anym = pl.BlockSpec(memory_space=pl.ANY)
    dma = pltpu.SemaphoreType.DMA
    plane2 = [dma((np_,)), dma((np_,))]
    line2 = [dma((nd,)), dma((nd,))]
    out, sd, su = pl.pallas_call(
        functools.partial(kernel, (nf, nd, ne, seqs, groups)),
        out_shape=(
            jax.ShapeDtypeStruct((tok, model), BF16),
            jax.ShapeDtypeStruct((rank, width), F32),
            jax.ShapeDtypeStruct((rank, values), F32),
        ),
        in_specs=[anym, anym, vmem, vmem, vmem, anym, anym, anym],
        out_specs=(anym, vmem, vmem),
        scratch_shapes=[
            pltpu.VMEM((tok, model), BF16),
            pltpu.VMEM((cols, values), BF16),
            pltpu.VMEM((rank, values), BF16),
            pltpu.VMEM((nd, 8, LANES), F32),
            pltpu.VMEM((np_, nd, 8, LANES), F32),
            pltpu.VMEM((np_, nd, LANES), F32),
            pltpu.VMEM((np_, tok, values), BF16),
            pltpu.VMEM((nf, rank, width), BF16),
            pltpu.VMEM((tok, values), BF16),
            pltpu.VMEM((np_, rank, cols), BF16),
            pltpu.VMEM((np_, rank, cols), BF16),
            pltpu.VMEM((np_, rank, cols), BF16),
            pltpu.VMEM((np_, 8, values), F32),
            pltpu.VMEM((np_, 8, values), F32),
            pltpu.VMEM((np_, 8, values), F32),
            pltpu.VMEM((nd, rank, cols), BF16),
            pltpu.VMEM((nd, 8, values), F32),
            pltpu.VMEM((ne, rank, cols), BF16),
            pltpu.VMEM((np_, 8, values + LANES), F32),
            pltpu.VMEM((np_, tok, cols), BF16),
            dma((6,)),
        ]
        + line2
        + plane2
        + plane2
        + [dma((nf,)), dma((nf,))]
        + plane2
        + plane2
        + plane2
        + plane2
        + line2
        + line2
        + [dma((ne,)), dma((ne,))]
        + plane2
        + plane2,
        compiler_params=pltpu.CompilerParams(
            collective_id=0, has_side_effects=True, vmem_limit_bytes=60 * 1024 * 1024
        ),
        cost_estimate=pl.CostEstimate(
            flops=4 * tok * model * values, bytes_accessed=6 * tok * model, transcendentals=0
        ),
    )(
        activations,
        upstream,
        reward.reshape(1, seqs),
        prompt_group_index.reshape(1, seqs),
        segment,
        frozen_value_weight,
        adapter_down_weight.T,
        adapter_up_weight,
    )
    return out, sd.T, su


def solution(mesh):
    everything = ("fsdp", "dp", "engine")
    return jax.shard_map(
        local,
        mesh=mesh,
        in_specs=(
            P(everything, None),
            P(everything, None),
            P(everything, None),
            P(everything),
            P(everything, None),
            P(("fsdp", "engine"), None),
            P("fsdp", None),
            P(),
        ),
        out_specs=(P(everything, None), P("fsdp", None), P()),
        check_vma=False,
    )
```
